512 devices in a mesh: clip: 128 (over z, x_hi, y), space: 4 (over x_lo, core).
Axes of the slice: x: 4 (x_hi: 2, x_lo: 2; x = x_hi * 2 + x_lo), y: 8, z: 8, core: 2. Of those that a mesh axis runs over, the one named last changes fastest.
Arguments:
- tokens: bfloat16 [2048, 96, 1280], P('clip', 'space'), may hold values from -8 to 8, as said below
- w_query: bfloat16 [1280, 640], P('space'), may hold values from -0.4472136 to 0.4472136
- w_key: bfloat16 [1280, 640], P('space'), may hold values from -0.4472136 to 0.4472136
- w_value: bfloat16 [1280, 640], P('space'), may hold values from -0.15625 to 0.15625
- w_out: bfloat16 [640, 1280], P('space'), may hold values from -0.25 to 0.25
- halo_width: int32 [128], P('clip'), may hold values from 1 to 4, as said below
- global_frame: int32 [128], P('clip'), may hold values from 0 to 15
Outputs:
- attended_out: bfloat16 [2048, 96, 1280], P('clip', 'space')
The draws below stay inside these ranges and needn't reach their ends.
Inputs may be any that keep to these rules, and one draw needn't show every extreme that they name: tokens of order one. `halo_width`: some clip has exactly 4.
All inputs are finite; a program needn't handle non-finite values.
Results may differ from the reference program's by a relative error of at most 0.0075.
Values may be sent and summed in bfloat16 or wider, within the bound.
A program may use at most 64 MiB of HBM per device.

```python
import math
import jax
import jax.numpy as jnp
from jax import lax

C = 1280
HEADS = 10
HDIM = 64
FRAMES = 16
HALO = 4
INNER = 640
CLIPS = 128
FRAMES_ALL = 2048
POSITIONS = 96


def draw_w_query(key, part):
    key = jax.random.fold_in(key, 5)
    fresh = jnp.clip(jax.random.normal(key, (C, INNER), jnp.float32), -3.0, 3.0)
    return (fresh / math.sqrt(C)).astype(jnp.bfloat16)


def draw_w_key(key, part):
    key = jax.random.fold_in(key, 7)
    fresh = jnp.clip(jax.random.normal(key, (C, INNER), jnp.float32), -3.0, 3.0)
    return (fresh / math.sqrt(C)).astype(jnp.bfloat16)


def draw_tokens(key, part):
    key = jax.random.fold_in(key, 3)
    first_key = jax.random.fold_in(key, 0)
    return jnp.clip(jax.random.normal(first_key, (FRAMES_ALL, POSITIONS, C), jnp.float32), -4.0, 4.0).astype(jnp.bfloat16)


def draw_halo_width(key, part):
    key = jax.random.fold_in(key, 11)
    first_key, second_key = jax.random.split(key)
    widths = jax.random.randint(first_key, (CLIPS,), 1, HALO + 1).astype(jnp.int32)
    chosen = jax.random.randint(second_key, (), 0, CLIPS)
    return jnp.where(jnp.arange(CLIPS) == chosen, HALO, widths).astype(jnp.int32)


def touch_ends(drawn, key, least, high):
    spot = [jax.random.randint(jax.random.fold_in(key, axis), (), 0, length) for axis, length in enumerate(drawn.shape)]
    longest = drawn.shape.index(max(drawn.shape))
    beside = spot[:longest] + [(spot[longest] + 1) % drawn.shape[longest]] + spot[longest + 1:]
    return drawn.at[tuple(spot)].set(least).at[tuple(beside)].set(high)


def shard_levels(stream_key, shape, pieces, least, largest):
    def one(dim, shards_of):
        steps = jax.random.uniform(jax.random.fold_in(jax.random.fold_in(stream_key, 6), dim), (shards_of,), jnp.float32, least / len(pieces), largest / len(pieces))
        return jnp.repeat(jnp.exp(steps), shape[dim] // shards_of).reshape((-1,) + (1,) * (len(shape) - dim - 1))

    gain = one(*pieces[0])
    for cut in pieces[1:]:
        gain = gain * one(*cut)
    return gain


def centred(rng, extent, width, bound, cuts=(), kind=jnp.bfloat16):
    level = shard_levels(rng, extent, cuts, -0.22, 0.18) if cuts else 1.0
    values = jax.random.normal(rng, extent, jnp.float32) * width * level
    return jnp.minimum(jnp.maximum(values, -bound), bound).astype(kind)


def setup_inputs(seed: int = 0) -> dict:
    arg_keys = jax.random.split(jax.random.key(seed), 8)
    return {
        "tokens": draw_tokens(jax.random.fold_in(arg_keys[7], 71), 0),
        "w_query": draw_w_query(jax.random.fold_in(arg_keys[7], 71), 0),
        "w_key": draw_w_key(jax.random.fold_in(arg_keys[7], 71), 0),
        "w_value": centred(arg_keys[3], (C, INNER), C ** -0.5, 0.15625, ((0, 4),)),
        "w_out": centred(arg_keys[4], (INNER, C), INNER ** -0.5, 0.25, ((0, 4),)),
        "halo_width": draw_halo_width(jax.random.fold_in(arg_keys[7], 71), 0),
        "global_frame": touch_ends(jax.random.randint(arg_keys[6], (CLIPS,), 0, FRAMES), jax.random.fold_in(arg_keys[6], 1), 0, FRAMES - 1).astype(jnp.int32),
    }


def reference(tokens, w_query, w_key, w_value, w_out, halo_width, global_frame):
    frame_total, place_count, model_width = tokens.shape
    flat_rows = tokens.reshape(frame_total * place_count, model_width)

    def project(weight):
        done = jnp.dot(flat_rows, weight, preferred_element_type=jnp.float32).astype(jnp.bfloat16)
        return done.reshape(frame_total, place_count, HEADS, HDIM)
    queries = project(w_query)
    keys_all = project(w_key)
    values_all = project(w_value)
    clip_count = frame_total // FRAMES
    picked = jnp.arange(clip_count).astype(jnp.int32) * FRAMES + global_frame.astype(jnp.int32)
    pool_keys = keys_all[picked]
    pool_values = values_all[picked]
    margin = jnp.zeros((HALO, place_count, HEADS, HDIM), jnp.bfloat16)
    padded_keys = jnp.concatenate([margin, keys_all, margin], axis=0)
    padded_values = jnp.concatenate([margin, values_all, margin], axis=0)
    score_scale = 1.0 / math.sqrt(HDIM)
    key_slot = jnp.arange(FRAMES + 2 * HALO + clip_count).astype(jnp.int32)

    def one_clip(clip_index):
        first_row = (clip_index * FRAMES).astype(jnp.int32)
        clip_queries = lax.dynamic_slice_in_dim(queries, first_row, FRAMES, 0)
        near_keys = lax.dynamic_slice_in_dim(padded_keys, first_row, FRAMES + 2 * HALO, 0)
        near_values = lax.dynamic_slice_in_dim(padded_values, first_row, FRAMES + 2 * HALO, 0)
        cand_keys = jnp.concatenate([near_keys, pool_keys], axis=0).astype(jnp.float32)
        cand_values = jnp.concatenate([near_values, pool_values], axis=0).astype(jnp.float32)
        scores = jnp.einsum('fphd,gphd->phfg', clip_queries.astype(jnp.float32), cand_keys) * score_scale
        reach_width = halo_width[clip_index]
        before_mask = (key_slot < HALO) & (clip_index > 0) & (HALO - key_slot <= reach_width)
        after_mask = (key_slot >= FRAMES + HALO) & (key_slot < FRAMES + 2 * HALO) & (clip_index < clip_count - 1) & (key_slot - FRAMES - HALO + 1 <= reach_width)
        inside_mask = (key_slot >= HALO) & (key_slot < FRAMES + HALO) | (key_slot >= FRAMES + 2 * HALO)
        valid_key = before_mask | after_mask | inside_mask
        scores = jnp.where(valid_key, scores, -1e+30)
        row_top = lax.optimization_barrier(jnp.max(scores, axis=-1, keepdims=True))
        expos = jnp.where(valid_key, jnp.exp(scores - row_top), 0.0)
        weights = (expos / lax.optimization_barrier(jnp.sum(expos, axis=-1, keepdims=True))).astype(jnp.bfloat16)
        mixed = jnp.einsum('phfg,gphd->fphd', weights.astype(jnp.float32), cand_values)
        return mixed.astype(jnp.bfloat16)
    attended = lax.map(one_clip, jnp.arange(clip_count).astype(jnp.int32))
    attended = attended.reshape(frame_total * place_count, HEADS * HDIM)
    result = jnp.dot(attended, w_out, preferred_element_type=jnp.float32).astype(jnp.bfloat16)
    return result.reshape(frame_total, place_count, model_width)
```

```python
import jax
import jax.numpy as jnp
from jax import lax
from jax.experimental import pallas as pl
from jax.experimental.pallas import tpu as pltpu
from jax.sharding import PartitionSpec as P

MESH = pl.DeviceIdType.MESH
BF = jnp.bfloat16
F32 = jnp.float32

RING = 8
C = 1280
INNER = 640
FRAMES = 16
PLACES = 24
ROWS = FRAMES * PLACES
HALO = 4
PAIRS = 5
SCALE = 0.125
LOW = -1e30
PARTS = ((0, 2), (16, 1))
SPOTS = ((0, 0), (0, 1), (1, 0))
WIDE = INNER + 128


def iota(shape, dim):
    return lax.broadcasted_iota(jnp.int32, shape, dim)


def onehot(mask):
    return jnp.where(mask, 1.0, 0.0).astype(BF)


def dot(a, b):
    return jnp.dot(a, b, preferred_element_type=F32)


def dot_t(a, b):
    return lax.dot_general(a, b, (((1,), (1,)), ((), ())), preferred_element_type=F32)


def kernel(
    tok_hbm, wq_hbm, wk_hbm, wv_hbm, wo_hbm, halo_s, gf_s, out_ref,
    tok, xt, htok, xht, wq, wk, wv, wo, q_own, qz, qy, k_own, v_own, k_mar, v_mar, k_pool, v_pool,
    mz, my, rz, ry, poolz, pooly, obuf, og, near_o, near_l, att,
    loc_sem, w_send, w_recv, h_send, h_recv, m_send, m_recv, r_send, r_recv, q_send, q_recv, o_send, o_recv,
):
    c = lax.axis_index("clip")
    s = lax.axis_index("space")
    z, xh, y = c // 16, (c // 8) % 2, c % 8
    xl, core = s // 2, s % 2
    x = xh * 2 + xl

    def dev(z_, xh_, y_, s_):
        return (z_ * 16 + xh_ * 8 + y_, s_)

    mate = (c, xl * 2 + 1 - core)
    up = (x + 1) % 4
    down = (x + 3) % 4
    x_up = dev(z, up // 2, y, (up % 2) * 2 + core)
    x_down = dev(z, down // 2, y, (down % 2) * 2 + core)
    clip_next = ((c + 1) % 128, s)
    clip_prev = ((c + 127) % 128, s)
    own = (z, y)
    across = (y, z)

    def ring_dev(part, place, xh_):
        return dev(place, xh_, y, s) if part == 0 else dev(z, xh_, place, s)

    def cross_dev(part, place):
        return dev(z, xh, place, s) if part == 0 else dev(place, xh, y, s)

    weights = ((wq_hbm, wq), (wk_hbm, wk), (wv_hbm, wv), (wo_hbm, wo))
    tok_in = pltpu.make_async_copy(tok_hbm, tok, loc_sem.at[0])
    tok_in.start()

    def shard(i, index, half=None):
        full = weights[i][1]
        rows = full.shape[0] // 4
        if half is None:
            return full.at[pl.ds(pl.multiple_of(index * rows, 16), rows)]
        return full.at[pl.ds(pl.multiple_of(index * rows + half * (rows // 2), 16), rows // 2)]

    w_in = []
    for i in range(4):
        copy = pltpu.make_async_copy(weights[i][0], shard(i, s), loc_sem.at[1 + i])
        copy.start()
        w_in.append(copy)

    barrier = pltpu.get_barrier_semaphore()

    def greet(device):
        pl.semaphore_signal(barrier, inc=1, device_id=device, device_id_type=MESH)

    for part in range(2):
        def greet_same(d, carry, part=part):
            greet(ring_dev(part, (own[part] + d) % RING, xh))
            return carry

        def greet_other(d, carry, part=part):
            greet(ring_dev(part, (own[part] + d) % RING, 1 - xh))
            return carry

        lax.fori_loop(1, RING, greet_same, 0)
        lax.fori_loop(0, RING, greet_other, 0)
    for device in (mate, x_up, x_down, clip_next, clip_prev):
        greet(device)

    tok_in.wait()
    frame = gf_s[0]
    pick = onehot(iota((PLACES, ROWS), 1) == iota((PLACES, ROWS), 0) + frame * PLACES)
    picked = dot(pick, tok[...]).astype(BF)
    for part, buf in ((0, mz), (1, my)):
        first, count = PARTS[part]
        shape = (RING * 16, PLACES)
        spot = iota(shape, 1) - first - (iota(shape, 0) >> 4) * count
        row = iota(shape, 0) & 15
        inside = (spot >= 0) & (spot < count)
        total = jnp.zeros((RING * 16, 256), F32)
        for j in range(5):
            choose = onehot(inside & (row == spot * 5 + j))
            total = total + dot(choose, picked[:, 256 * j : 256 * j + 256])
        buf[...] = total.astype(BF).reshape(RING, 16, 256)

    pl.semaphore_wait(barrier, 2 * (2 * RING - 1) + 5)

    def message(part, d, other):
        send, land = ((mz, rz), (my, ry))[part]
        place = (own[part] + d) % RING
        xh_ = 1 - xh if other else xh
        k = d + (RING if other else 0)
        return pltpu.make_async_remote_copy(
            src_ref=send.at[place],
            dst_ref=land.at[xh * RING + own[part]],
            send_sem=m_send.at[part, k],
            recv_sem=m_recv.at[part, k],
            device_id=ring_dev(part, place, xh_),
            device_id_type=MESH,
        )

    def each_message(act):
        for part in range(2):
            def same(d, carry, part=part):
                act(message(part, d, False))
                return carry

            def other(d, carry, part=part):
                act(message(part, d, True))
                return carry

            lax.fori_loop(1, RING, same, 0)
            lax.fori_loop(0, RING, other, 0)

    def weight_copy(i, kind):
        rows = weights[i][0].shape[0]
        theirs = (1 - xl) * 2 + core
        if kind == 0:
            src, dst, device = weights[i][0].at[pl.ds(0, rows // 2)], shard(i, s, 0), x_up
        elif kind == 1:
            src, dst, device = weights[i][0].at[pl.ds(rows // 2, rows // 2)], shard(i, s, 1), x_down
        elif kind == 2:
            src, dst, device = weights[i][0], shard(i, s), mate
        else:
            src, dst, device = shard(i, theirs, kind - 3), shard(i, theirs, kind - 3), mate
        return pltpu.make_async_remote_copy(
            src_ref=src, dst_ref=dst, send_sem=w_send.at[i, kind], recv_sem=w_recv.at[i, kind],
            device_id=device, device_id_type=MESH,
        )

    def margin_copy(side):
        edge = HALO * PLACES
        src = tok_hbm.at[pl.ds(ROWS - edge, edge)] if side == 0 else tok_hbm.at[pl.ds(0, edge)]
        return pltpu.make_async_remote_copy(
            src_ref=src,
            dst_ref=htok.at[pl.ds(side * edge, edge)],
            send_sem=h_send.at[side],
            recv_sem=h_recv.at[side],
            device_id=clip_next if side == 0 else clip_prev,
            device_id_type=MESH,
        )

    each_message(lambda copy: copy.start())
    for kind in range(3):
        weight_copy(0, kind).start()
    for side in range(2):
        margin_copy(side).start()
    for i in range(1, 4):
        for kind in range(3):
            weight_copy(i, kind).start()

    shape = (ROWS, ROWS)
    turn = onehot(iota(shape, 1) == (iota(shape, 0) & 15) * PLACES + (iota(shape, 0) >> 4))
    xt[...] = dot(turn, tok[...]).astype(BF)

    rz[xh * RING + z] = mz[z]
    ry[xh * RING + y] = my[y]
    each_message(lambda copy: copy.wait_recv())
    pools = (poolz, pooly)
    for part, land in ((0, rz), (1, ry)):
        count = PARTS[part][1]
        shape = (count * 16, 256)
        r, col = iota(shape, 0), iota(shape, 1)
        for j in range(5):
            choose = onehot(((r & 15) == (col >> 4)) & ((col & 15) == (r >> 4) * 5 + j))
            block = dot(choose, land[...].reshape(256, 256)).astype(BF)
            pools[part][across[part], :, :, 256 * j : 256 * j + 256] = block.reshape(count, 16, 256)

    def ring_copy(part, way, step):
        b = across[part]
        pool = pools[part]
        if way == 0:
            origin, device = (b + RING - step) % RING, cross_dev(part, (b + 1) % RING)
        else:
            origin, device = (b + step) % RING, cross_dev(part, (b + RING - 1) % RING)
        block = pool.at[origin]
        if step == 3 and part == 0:
            block = pool.at[origin, way]
        return pltpu.make_async_remote_copy(
            src_ref=block, dst_ref=block, send_sem=r_send.at[part, way, step], recv_sem=r_recv.at[part, way, step],
            device_id=device, device_id_type=MESH,
        )

    def ring_pieces(step):
        if step < 3:
            return ((0, 0), (0, 1), (1, 0), (1, 1))
        return ((0, 0), (0, 1), (1, 0))

    def ring_step(step):
        for part, way in ring_pieces(step):
            if step > 0:
                ring_copy(part, way, step - 1).wait_recv()
            ring_copy(part, way, step).start()
        if step == 3:
            ring_copy(1, 1, 2).wait_recv()

    def pass_on(i):
        weight_copy(i, 0).wait_recv()
        weight_copy(i, 3).start()
        weight_copy(i, 1).wait_recv()
        weight_copy(i, 4).start()

    def whole(i):
        w_in[i].wait()
        for kind in range(2, 5):
            weight_copy(i, kind).wait_recv()

    ring_step(0)

    pass_on(0)
    whole(0)
    q_own[...] = (dot(xt[...], wq[...]) * SCALE).astype(BF)

    def query_copy(part, d):
        first, count = PARTS[part]
        place = (own[part] + d) % RING
        rows = count * 16
        return pltpu.make_async_remote_copy(
            src_ref=q_own.at[pl.ds(pl.multiple_of(first * 16 + place * rows, 16), rows)],
            dst_ref=(qz, qy)[part].at[own[part]],
            send_sem=q_send.at[part, d],
            recv_sem=q_recv.at[part, d],
            device_id=ring_dev(part, place, xh),
            device_id_type=MESH,
        )

    def each_query(act):
        for part in range(2):
            def one(d, carry, part=part):
                act(query_copy(part, d))
                return carry

            lax.fori_loop(1, RING, one, 0)

    each_query(lambda copy: copy.start())
    qz[z] = q_own[pl.ds(pl.multiple_of(z * 32, 16), 32)]
    qy[y] = q_own[pl.ds(pl.multiple_of(256 + y * 16, 16), 16)]
    ring_step(1)

    for side in range(2):
        margin_copy(side).wait_recv()
    edge = 2 * HALO * PLACES
    shape = (edge, edge)
    turn = onehot(iota(shape, 1) == (iota(shape, 0) & 7) * PLACES + (iota(shape, 0) >> 3))
    xht[...] = dot(turn, htok[...]).astype(BF)

    ring_step(2)
    pass_on(1)
    whole(1)
    k_own[...] = dot(xt[...], wk[...]).astype(BF)
    k_mar[...] = dot(xht[...], wk[...]).astype(BF)
    ring_step(3)
    pass_on(2)
    for part, way in ring_pieces(3):
        ring_copy(part, way, 3).wait_recv()
    for k, (part, p) in enumerate(SPOTS):
        k_pool[k] = dot(pools[part][:, p].reshape(RING * 16, C), wk[...]).astype(BF)
    whole(2)
    for k, (part, p) in enumerate(SPOTS):
        v_pool[k] = dot(pools[part][:, p].reshape(RING * 16, C), wv[...]).astype(BF)

    each_query(lambda copy: copy.wait_recv())
    lane = iota((128, 128), 1)
    left = lane < 64
    left_b = onehot(iota((1, 128), 1) < 64)
    right_b = onehot(iota((1, 128), 1) >= 64)

    def reply_copy(k, d):
        part, p = SPOTS[k]
        first, count = PARTS[part]
        place = (own[part] + d) % RING
        return pltpu.make_async_remote_copy(
            src_ref=obuf.at[k, place],
            dst_ref=og.at[pl.ds(pl.multiple_of((first + own[part] * count + p) * 16, 16), 16)],
            send_sem=o_send.at[k, d],
            recv_sem=o_recv.at[k, d],
            device_id=ring_dev(part, place, xh),
            device_id_type=MESH,
        )

    def each_reply(k, act):
        def one(d, carry):
            act(reply_copy(k, d))
            return carry

        lax.fori_loop(1, RING, one, 0)

    for k, (part, p) in enumerate(SPOTS):
        first, count = PARTS[part]
        queries = (qz, qy)[part]
        logs = jnp.zeros((128, 128), F32)
        for pair in range(PAIRS):
            lanes = slice(128 * pair, 128 * pair + 128)
            q = queries[:, 16 * p : 16 * p + 16, lanes].reshape(128, 128)
            keys = k_pool[k, :, lanes]
            values = v_pool[k, :, lanes]
            scores = dot_t(q, jnp.concatenate([keys * left_b, keys * right_b], axis=0))
            s0, s1 = scores[:, :128], scores[:, 128:]
            m0 = jnp.max(s0, axis=1, keepdims=True)
            m1 = jnp.max(s1, axis=1, keepdims=True)
            e0 = jnp.exp(s0 - m0)
            e1 = jnp.exp(s1 - m1)
            l0 = jnp.sum(e0, axis=1, keepdims=True)
            l1 = jnp.sum(e1, axis=1, keepdims=True)
            mixed = dot(
                jnp.concatenate([e0.astype(BF), e1.astype(BF)], axis=1),
                jnp.concatenate([values * left_b, values * right_b], axis=0),
            )
            mixed = mixed * jnp.where(left, 1.0 / l0, 1.0 / l1)
            obuf[k, :, :, lanes] = mixed.astype(BF).reshape(RING, 16, 128)
            logs = jnp.where(lane == 2 * pair, m0 + jnp.log(l0), logs)
            logs = jnp.where(lane == 2 * pair + 1, m1 + jnp.log(l1), logs)
        high = logs.astype(BF).astype(F32)
        middle = (logs - high).astype(BF).astype(F32)
        low = (logs - high - middle).astype(BF).astype(F32)
        packed = high + pltpu.roll(middle, 16, 1) + pltpu.roll(low, 32, 1)
        obuf[k, :, :, INNER:] = packed.astype(BF).reshape(RING, 16, 128)
        each_reply(k, lambda copy: copy.start())
        og[pl.ds(pl.multiple_of((first + own[part] * count + p) * 16, 16), 16)] = obuf[k, own[part]]

    pass_on(3)

    v_own[...] = dot(xt[...], wv[...]).astype(BF)
    v_mar[...] = dot(xht[...], wv[...]).astype(BF)
    row8 = iota((128, 128), 0) >> 4
    own_bias = jnp.where(row8 == (lane >> 4), 0.0, LOW)
    half = lane & 63
    slot = half & 7
    reach = halo_s[0]
    before = (slot < HALO) & (c > 0) & (HALO - slot <= reach)
    after = (slot >= HALO) & (c < 127) & (slot - HALO + 1 <= reach)
    mar_bias = jnp.where((row8 == (half >> 3)) & (before | after), 0.0, LOW)
    for g in range(3):
        rows = slice(128 * g, 128 * g + 128)
        edges = slice(64 * g, 64 * g + 64)
        logs = jnp.zeros((128, 128), F32)
        for pair in range(PAIRS):
            lanes = slice(128 * pair, 128 * pair + 128)
            q = q_own[rows, lanes]
            ko, vo, km, vm = k_own[rows, lanes], v_own[rows, lanes], k_mar[edges, lanes], v_mar[edges, lanes]
            scores = dot_t(q, jnp.concatenate([ko * left_b, ko * right_b, km * left_b, km * right_b], axis=0))
            s0 = scores[:, :128] + own_bias
            s1 = scores[:, 128:256] + own_bias
            sm = scores[:, 256:] + mar_bias
            m0 = jnp.max(jnp.maximum(s0, jnp.where(left, sm, LOW)), axis=1, keepdims=True)
            m1 = jnp.max(jnp.maximum(s1, jnp.where(left, LOW, sm)), axis=1, keepdims=True)
            e0 = jnp.exp(s0 - m0)
            e1 = jnp.exp(s1 - m1)
            em = jnp.exp(sm - jnp.where(left, m0, m1))
            l0 = jnp.sum(e0 + jnp.where(left, em, 0.0), axis=1, keepdims=True)
            l1 = jnp.sum(e1 + jnp.where(left, 0.0, em), axis=1, keepdims=True)
            mixed = dot(
                jnp.concatenate([e0.astype(BF), e1.astype(BF), em.astype(BF)], axis=1),
                jnp.concatenate([vo * left_b, vo * right_b, vm * left_b, vm * right_b], axis=0),
            )
            near_o[rows, lanes] = mixed * jnp.where(left, 1.0 / l0, 1.0 / l1)
            logs = jnp.where(lane == 2 * pair, m0 + jnp.log(l0), logs)
            logs = jnp.where(lane == 2 * pair + 1, m1 + jnp.log(l1), logs)
        near_l[rows, :] = logs

    for k in range(3):
        each_reply(k, lambda copy: copy.wait_recv())
    r128, c128 = iota((128, 128), 0), iota((128, 128), 1)
    gather_logs = onehot(((r128 & 15) == c128) & (r128 < 48) & (c128 < 10))
    expand = onehot(iota((128, INNER), 0) == (iota((128, INNER), 1) >> 6))
    for g in range(3):
        rows = slice(128 * g, 128 * g + 128)
        far_l = dot(og[rows, INNER:], gather_logs)
        share = 1.0 / (1.0 + jnp.exp(near_l[rows, :] - far_l))
        high = share.astype(BF)
        rest = (share - high.astype(F32)).astype(BF)
        wide = dot(high, expand) + dot(rest, expand)
        near = near_o[rows, :]
        att[rows, :] = (near + wide * (og[rows, :INNER].astype(F32) - near)).astype(BF)
    shape = (ROWS, ROWS)
    turn = onehot(iota(shape, 0) == (iota(shape, 1) & 15) * PLACES + (iota(shape, 1) >> 4))
    ordered = dot(turn, att[...]).astype(BF)
    whole(3)
    out_ref[...] = dot(ordered, wo[...]).astype(BF)

    each_message(lambda copy: copy.wait_send())
    for i in range(4):
        for kind in range(5):
            weight_copy(i, kind).wait_send()
    for side in range(2):
        margin_copy(side).wait_send()
    for step in range(4):
        for part, way in ring_pieces(step):
            ring_copy(part, way, step).wait_send()
    each_query(lambda copy: copy.wait_send())
    for k in range(3):
        each_reply(k, lambda copy: copy.wait_send())


def body(tokens, w_query, w_key, w_value, w_out, halo_width, global_frame):
    rows = tokens.reshape(ROWS, C)
    any_spec = pl.BlockSpec(memory_space=pl.ANY)
    smem = pl.BlockSpec(memory_space=pltpu.SMEM)
    v = pltpu.VMEM
    dma = pltpu.SemaphoreType.DMA
    edge = 2 * HALO * PLACES
    out = pl.pallas_call(
        kernel,
        out_shape=jax.ShapeDtypeStruct((ROWS, C), BF),
        in_specs=[any_spec] * 5 + [smem] * 2,
        out_specs=pl.BlockSpec(memory_space=pltpu.VMEM),
        scratch_shapes=[
            v((ROWS, C), BF), v((ROWS, C), BF), v((edge, C), BF), v((edge, C), BF),
            v((C, INNER), BF), v((C, INNER), BF), v((C, INNER), BF), v((INNER, C), BF),
            v((ROWS, INNER), BF), v((RING, 32, INNER), BF), v((RING, 16, INNER), BF),
            v((ROWS, INNER), BF), v((ROWS, INNER), BF), v((edge, INNER), BF), v((edge, INNER), BF),
            v((3, 128, INNER), BF), v((3, 128, INNER), BF),
            v((RING, 16, 256), BF), v((RING, 16, 256), BF), v((16, 16, 256), BF), v((16, 16, 256), BF),
            v((RING, 2, 16, C), BF), v((RING, 1, 16, C), BF),
            v((3, RING, 16, WIDE), BF), v((ROWS, WIDE), BF),
            v((ROWS, INNER), F32), v((ROWS, 128), F32), v((ROWS, INNER), BF),
            dma((5,)), dma((4, 5)), dma((4, 5)), dma((2,)), dma((2,)), dma((2, 16)), dma((2, 16)),
            dma((2, 2, 4)), dma((2, 2, 4)), dma((2, 8)), dma((2, 8)), dma((3, 8)), dma((3, 8)),
        ],
        compiler_params=pltpu.CompilerParams(
            collective_id=0, has_side_effects=True, vmem_limit_bytes=48 * 1024 * 1024
        ),
    )(rows, w_query, w_key, w_value, w_out, halo_width, global_frame)
    return out.reshape(FRAMES, PLACES, C)


def solution(mesh):
    return jax.shard_map(
        body,
        mesh=mesh,
        in_specs=(
            P("clip", "space", None),
            P("space", None),
            P("space", None),
            P("space", None),
            P("space", None),
            P("clip"),
            P("clip"),
        ),
        out_specs=P("clip", "space", None),
        check_vma=False,
    )
```

```python
import jax
import jax.numpy as jnp
from jax import lax
from jax.experimental import pallas as pl
from jax.experimental.pallas import tpu as pltpu
from jax.sharding import PartitionSpec as P

MESH = pl.DeviceIdType.MESH
BF = jnp.bfloat16
F32 = jnp.float32

RING = 8
C = 1280
INNER = 640
FRAMES = 16
PLACES = 24
ROWS = FRAMES * PLACES
HALO = 4
PAIRS = 5
SCALE = 0.125
LOW = -1e30
GROUP = 16
WIDE = INNER + 128


def iota(shape, dim):
    return lax.broadcasted_iota(jnp.int32, shape, dim)


def onehot(mask):
    return jnp.where(mask, 1.0, 0.0).astype(BF)


def dot(a, b):
    return jnp.dot(a, b, preferred_element_type=F32)


def dot_t(a, b):
    return lax.dot_general(a, b, (((1,), (1,)), ((), ())), preferred_element_type=F32)


def rem(value, size):
    return lax.rem(value, jnp.int32(size))


def kernel(
    tok_hbm, wq_hbm, wk_hbm, wv_hbm, wo_hbm, halo_s, gf_s, out_ref,
    tok, xt, htok, xht, wq, wk, wv, wo, q_own, qz, qy, k_own, v_own, k_mar, v_mar, k_pool, v_pool,
    mine, rz, ry, poolz, pooly, oz, oy, og, near_o, near_l, att,
    loc_sem, w_send, w_recv, h_send, h_recv, m_send, m_recv, r_send, r_recv, q_send, q_recv, o_send, o_recv,
):
    c = lax.axis_index("clip")
    s = lax.axis_index("space")
    z, xh, y = lax.div(c, jnp.int32(16)), rem(lax.div(c, jnp.int32(8)), 2), rem(c, 8)
    xl, core = lax.div(s, jnp.int32(2)), rem(s, 2)
    x = xh * 2 + xl
    spot = xh * 8 + z

    def dev(z_, xh_, y_, s_):
        return (z_ * 16 + xh_ * 8 + y_, s_)

    mate = (c, xl * 2 + 1 - core)
    up = rem(x + 1, 4)
    down = rem(x + 3, 4)
    x_up = dev(z, lax.div(up, jnp.int32(2)), y, rem(up, 2) * 2 + core)
    x_down = dev(z, lax.div(down, jnp.int32(2)), y, rem(down, 2) * 2 + core)
    clip_next = (rem(c + 1, 128), s)
    clip_prev = (rem(c + 127, 128), s)

    def loop(start, stop, act):
        def step(d, carry):
            act(d)
            return carry

        lax.fori_loop(start, stop, step, 0)

    def group_dev(place):
        return dev(rem(place, 8), lax.div(place, jnp.int32(8)), y, s)

    weights = ((wq_hbm, wq), (wk_hbm, wk), (wv_hbm, wv), (wo_hbm, wo))
    tok_in = pltpu.make_async_copy(tok_hbm, tok, loc_sem.at[0])
    tok_in.start()
    barrier = pltpu.get_barrier_semaphore()

    def greet(device):
        pl.semaphore_signal(barrier, inc=1, device_id=device, device_id_type=MESH)

    for device in (mate, x_up, x_down, clip_next, clip_prev):
        greet(device)
    loop(1, GROUP, lambda d: greet(group_dev(rem(spot + d, GROUP))))
    loop(1, RING, lambda d: greet(dev(z, xh, rem(y + d, RING), s)))
    loop(0, RING, lambda d: greet(dev(z, 1 - xh, rem(y + d, RING), s)))

    def shard(i, index, half=None):
        full = weights[i][1]
        rows = full.shape[0] // 4
        if half is None:
            return full.at[pl.ds(pl.multiple_of(index * rows, 16), rows)]
        return full.at[pl.ds(pl.multiple_of(index * rows + half * (rows // 2), 16), rows // 2)]

    w_in = []
    for i in range(4):
        copy = pltpu.make_async_copy(weights[i][0], shard(i, s), loc_sem.at[1 + i])
        copy.start()
        w_in.append(copy)

    def message(part, d):
        if part == 0:
            place = rem(spot + d, GROUP)
            src, dst, device = mine.at[place], rz.at[spot], group_dev(place)
        else:
            place = rem(y + d, RING)
            xh_ = rem(xh + lax.div(d, jnp.int32(8)), 2)
            src, dst, device = mine.at[16 + place], ry.at[xh * 8 + y], dev(z, xh_, place, s)
        return pltpu.make_async_remote_copy(
            src_ref=src, dst_ref=dst, send_sem=m_send.at[part, d], recv_sem=m_recv.at[part, d],
            device_id=device, device_id_type=MESH,
        )

    def each_message(act):
        for part in range(2):
            loop(1, 16, lambda d, part=part: act(message(part, d)))

    def weight_copy(i, kind):
        rows = weights[i][0].shape[0]
        theirs = (1 - xl) * 2 + core
        if kind == 0:
            src, dst, device = weights[i][0].at[pl.ds(0, rows // 2)], shard(i, s, 0), x_up
        elif kind == 1:
            src, dst, device = weights[i][0].at[pl.ds(rows // 2, rows // 2)], shard(i, s, 1), x_down
        elif kind == 2:
            src, dst, device = weights[i][0], shard(i, s), mate
        else:
            src, dst, device = shard(i, theirs, kind - 3), shard(i, theirs, kind - 3), mate
        return pltpu.make_async_remote_copy(
            src_ref=src, dst_ref=dst, send_sem=w_send.at[i, kind], recv_sem=w_recv.at[i, kind],
            device_id=device, device_id_type=MESH,
        )

    def margin_copy(side):
        edge = HALO * PLACES
        src = tok_hbm.at[pl.ds(ROWS - edge, edge)] if side == 0 else tok_hbm.at[pl.ds(0, edge)]
        return pltpu.make_async_remote_copy(
            src_ref=src,
            dst_ref=htok.at[pl.ds(side * edge, edge)],
            send_sem=h_send.at[side],
            recv_sem=h_recv.at[side],
            device_id=clip_next if side == 0 else clip_prev,
            device_id_type=MESH,
        )

    pools = (poolz, pooly)

    def block_copy(part, d):
        if part == 0:
            at, device = y, dev(z, xh, rem(y + d, RING), s)
        else:
            at, device = z, dev(rem(z + d, RING), xh, y, s)
        return pltpu.make_async_remote_copy(
            src_ref=pools[part].at[at], dst_ref=pools[part].at[at],
            send_sem=r_send.at[part, d], recv_sem=r_recv.at[part, d], device_id=device, device_id_type=MESH,
        )

    def each_block(act):
        for part in range(2):
            loop(1, RING, lambda d, part=part: act(block_copy(part, d)))

    def query_copy(part, d):
        if part == 0:
            place = rem(spot + d, GROUP)
            first, dst, device = place, qz.at[spot], group_dev(place)
        else:
            place = rem(y + d, RING)
            first, dst, device = 16 + place, qy.at[y], dev(z, xh, place, s)
        return pltpu.make_async_remote_copy(
            src_ref=q_own.at[pl.ds(pl.multiple_of(first * 16, 16), 16)], dst_ref=dst,
            send_sem=q_send.at[part, d], recv_sem=q_recv.at[part, d], device_id=device, device_id_type=MESH,
        )

    def each_query(act):
        loop(1, GROUP, lambda d: act(query_copy(0, d)))
        loop(1, RING, lambda d: act(query_copy(1, d)))

    def reply_copy(part, d):
        if part == 0:
            place = rem(spot + d, GROUP)
            src, first, device = oz.at[place], spot, group_dev(place)
        else:
            place = rem(y + d, RING)
            src, first, device = oy.at[place], 16 + y, dev(z, xh, place, s)
        return pltpu.make_async_remote_copy(
            src_ref=src, dst_ref=og.at[pl.ds(pl.multiple_of(first * 16, 16), 16)],
            send_sem=o_send.at[part, d], recv_sem=o_recv.at[part, d], device_id=device, device_id_type=MESH,
        )

    def each_reply(part, act):
        loop(1, (GROUP, RING)[part], lambda d: act(reply_copy(part, d)))

    pl.semaphore_wait(barrier, 15 + 7 + 8 + 5)
    for kind in range(3):
        weight_copy(0, kind).start()

    tok_in.wait()
    frame = gf_s[0]
    pick = onehot(iota((PLACES, ROWS), 1) == iota((PLACES, ROWS), 0) + frame * PLACES)
    picked = dot(pick, tok[...]).astype(BF)
    shape = (PLACES * 16, PLACES)
    match = iota(shape, 1) == (iota(shape, 0) >> 4)
    row = iota(shape, 0) & 15
    total = jnp.zeros((PLACES * 16, 128), F32)
    for j in range(10):
        total = total + dot(onehot(match & (row == j)), picked[:, 128 * j : 128 * j + 128])
    mine[...] = total.astype(BF).reshape(PLACES, 16, 128)
    each_message(lambda copy: copy.start())

    for side in range(2):
        margin_copy(side).start()
    for i in range(1, 4):
        for kind in range(3):
            weight_copy(i, kind).start()

    shape = (ROWS, ROWS)
    turn = onehot(iota(shape, 1) == (iota(shape, 0) & 15) * PLACES + (iota(shape, 0) >> 4))
    xt[...] = dot(turn, tok[...]).astype(BF)

    rz[spot] = mine[spot]
    ry[xh * 8 + y] = mine[16 + y]
    each_message(lambda copy: copy.wait_recv())
    r, col = iota((16, 256), 0), iota((16, 256), 1)
    for part, land, at in ((0, rz, y), (1, ry, z)):
        rows = land[...].reshape(256, 128)
        for j in range(10):
            choose = onehot((r == (col >> 4)) & ((col & 15) == j))
            pools[part][at, :, 128 * j : 128 * j + 128] = dot(choose, rows).astype(BF)
    each_block(lambda copy: copy.start())

    def pass_on(i):
        for half in range(2):
            weight_copy(i, half).wait_recv()
            weight_copy(i, 3 + half).start()

    def whole(i):
        w_in[i].wait()
        for kind in range(2, 5):
            weight_copy(i, kind).wait_recv()

    pass_on(0)
    whole(0)
    q_own[...] = (dot(xt[...], wq[...]) * SCALE).astype(BF)
    each_query(lambda copy: copy.start())
    qz[spot] = q_own[pl.ds(pl.multiple_of(spot * 16, 16), 16)]
    qy[y] = q_own[pl.ds(pl.multiple_of(256 + y * 16, 16), 16)]

    pass_on(1)
    whole(1)
    k_own[...] = dot(xt[...], wk[...]).astype(BF)
    each_block(lambda copy: copy.wait_recv())
    pass_on(2)
    for part in range(2):
        k_pool[part] = dot(pools[part][...].reshape(RING * 16, C), wk[...]).astype(BF)
    whole(2)
    for part in range(2):
        v_pool[part] = dot(pools[part][...].reshape(RING * 16, C), wv[...]).astype(BF)

    lane = iota((128, 128), 1)
    left = lane < 64
    left_b = onehot(iota((1, 128), 1) < 64)
    right_b = onehot(iota((1, 128), 1) >= 64)
    each_query(lambda copy: copy.wait_recv())

    def far(part, queries, out, start):
        logs = jnp.zeros((128, 128), F32)
        for pair in range(PAIRS):
            lanes = slice(128 * pair, 128 * pair + 128)
            q = queries[pl.ds(start, 8), :, lanes].reshape(128, 128)
            keys = k_pool[part, :, lanes]
            values = v_pool[part, :, lanes]
            scores = dot_t(q, jnp.concatenate([keys * left_b, keys * right_b], axis=0))
            s0, s1 = scores[:, :128], scores[:, 128:]
            m0 = jnp.max(s0, axis=1, keepdims=True)
            m1 = jnp.max(s1, axis=1, keepdims=True)
            e0 = jnp.exp(s0 - m0)
            e1 = jnp.exp(s1 - m1)
            l0 = jnp.sum(e0, axis=1, keepdims=True)
            l1 = jnp.sum(e1, axis=1, keepdims=True)
            mixed = dot(
                jnp.concatenate([e0.astype(BF), e1.astype(BF)], axis=1),
                jnp.concatenate([values * left_b, values * right_b], axis=0),
            )
            mixed = mixed * jnp.where(left, 1.0 / l0, 1.0 / l1)
            out[pl.ds(start, 8), :, lanes] = mixed.astype(BF).reshape(RING, 16, 128)
            logs = jnp.where(lane == 2 * pair, m0 + jnp.log(l0), logs)
            logs = jnp.where(lane == 2 * pair + 1, m1 + jnp.log(l1), logs)
        high = logs.astype(BF).astype(F32)
        middle = (logs - high).astype(BF).astype(F32)
        low = (logs - high - middle).astype(BF).astype(F32)
        packed = high + pltpu.roll(middle, 16, 1) + pltpu.roll(low, 32, 1)
        out[pl.ds(start, 8), :, INNER:] = packed.astype(BF).reshape(RING, 16, 128)

    for half in range(2):
        far(0, qz, oz, 8 * half)
    each_reply(0, lambda copy: copy.start())
    far(1, qy, oy, 0)
    each_reply(1, lambda copy: copy.start())
    og[pl.ds(pl.multiple_of(spot * 16, 16), 16)] = oz[spot]
    og[pl.ds(pl.multiple_of(256 + y * 16, 16), 16)] = oy[y]

    pass_on(3)

    for side in range(2):
        margin_copy(side).wait_recv()
    edge = 2 * HALO * PLACES
    shape = (edge, edge)
    turn = onehot(iota(shape, 1) == (iota(shape, 0) & 7) * PLACES + (iota(shape, 0) >> 3))
    xht[...] = dot(turn, htok[...]).astype(BF)
    k_mar[...] = dot(xht[...], wk[...]).astype(BF)
    v_mar[...] = dot(xht[...], wv[...]).astype(BF)
    v_own[...] = dot(xt[...], wv[...]).astype(BF)

    row8 = iota((128, 128), 0) >> 4
    own_bias = jnp.where(row8 == (lane >> 4), 0.0, LOW)
    half = lane & 63
    slot = half & 7
    reach = halo_s[0]
    before = (slot < HALO) & (c > 0) & (HALO - slot <= reach)
    after = (slot >= HALO) & (c < 127) & (slot - HALO + 1 <= reach)
    mar_bias = jnp.where((row8 == (half >> 3)) & (before | after), 0.0, LOW)
    for g in range(3):
        rows = slice(128 * g, 128 * g + 128)
        edges = slice(64 * g, 64 * g + 64)
        logs = jnp.zeros((128, 128), F32)
        for pair in range(PAIRS):
            lanes = slice(128 * pair, 128 * pair + 128)
            q = q_own[rows, lanes]
            ko, vo, km, vm = k_own[rows, lanes], v_own[rows, lanes], k_mar[edges, lanes], v_mar[edges, lanes]
            scores = dot_t(q, jnp.concatenate([ko * left_b, ko * right_b, km * left_b, km * right_b], axis=0))
            s0 = scores[:, :128] + own_bias
            s1 = scores[:, 128:256] + own_bias
            sm = scores[:, 256:] + mar_bias
            m0 = jnp.max(jnp.maximum(s0, jnp.where(left, sm, LOW)), axis=1, keepdims=True)
            m1 = jnp.max(jnp.maximum(s1, jnp.where(left, LOW, sm)), axis=1, keepdims=True)
            e0 = jnp.exp(s0 - m0)
            e1 = jnp.exp(s1 - m1)
            em = jnp.exp(sm - jnp.where(left, m0, m1))
            l0 = jnp.sum(e0 + jnp.where(left, em, 0.0), axis=1, keepdims=True)
            l1 = jnp.sum(e1 + jnp.where(left, 0.0, em), axis=1, keepdims=True)
            mixed = dot(
                jnp.concatenate([e0.astype(BF), e1.astype(BF), em.astype(BF)], axis=1),
                jnp.concatenate([vo * left_b, vo * right_b, vm * left_b, vm * right_b], axis=0),
            )
            near_o[rows, lanes] = mixed * jnp.where(left, 1.0 / l0, 1.0 / l1)
            logs = jnp.where(lane == 2 * pair, m0 + jnp.log(l0), logs)
            logs = jnp.where(lane == 2 * pair + 1, m1 + jnp.log(l1), logs)
        near_l[rows, :] = logs

    for part in range(2):
        each_reply(part, lambda copy: copy.wait_recv())
    r128, c128 = iota((128, 128), 0), iota((128, 128), 1)
    gather_logs = onehot(((r128 & 15) == c128) & (r128 < 48) & (c128 < 10))
    expand = onehot(iota((128, INNER), 0) == (iota((128, INNER), 1) >> 6))
    for g in range(3):
        rows = slice(128 * g, 128 * g + 128)
        far_l = dot(og[rows, INNER:], gather_logs)
        share = 1.0 / (1.0 + jnp.exp(near_l[rows, :] - far_l))
        high = share.astype(BF)
        rest = (share - high.astype(F32)).astype(BF)
        wide = dot(high, expand) + dot(rest, expand)
        near = near_o[rows, :]
        att[rows, :] = (near + wide * (og[rows, :INNER].astype(F32) - near)).astype(BF)
    shape = (ROWS, ROWS)
    turn = onehot(iota(shape, 0) == (iota(shape, 1) & 15) * PLACES + (iota(shape, 1) >> 4))
    ordered = dot(turn, att[...]).astype(BF)
    whole(3)
    out_ref[...] = dot(ordered, wo[...]).astype(BF)

    each_message(lambda copy: copy.wait_send())
    for i in range(4):
        for kind in range(5):
            weight_copy(i, kind).wait_send()
    for side in range(2):
        margin_copy(side).wait_send()
    each_block(lambda copy: copy.wait_send())
    each_query(lambda copy: copy.wait_send())
    for part in range(2):
        each_reply(part, lambda copy: copy.wait_send())


def body(tokens, w_query, w_key, w_value, w_out, halo_width, global_frame):
    rows = tokens.reshape(ROWS, C)
    any_spec = pl.BlockSpec(memory_space=pl.ANY)
    smem = pl.BlockSpec(memory_space=pltpu.SMEM)
    v = pltpu.VMEM
    dma = pltpu.SemaphoreType.DMA
    edge = 2 * HALO * PLACES
    out = pl.pallas_call(
        kernel,
        out_shape=jax.ShapeDtypeStruct((ROWS, C), BF),
        in_specs=[any_spec] * 5 + [smem] * 2,
        out_specs=pl.BlockSpec(memory_space=pltpu.VMEM),
        scratch_shapes=[
            v((ROWS, C), BF), v((ROWS, C), BF), v((edge, C), BF), v((edge, C), BF),
            v((C, INNER), BF), v((C, INNER), BF), v((C, INNER), BF), v((INNER, C), BF),
            v((ROWS, INNER), BF), v((GROUP, 16, INNER), BF), v((RING, 16, INNER), BF),
            v((ROWS, INNER), BF), v((ROWS, INNER), BF), v((edge, INNER), BF), v((edge, INNER), BF),
            v((2, 128, INNER), BF), v((2, 128, INNER), BF),
            v((PLACES, 16, 128), BF), v((GROUP, 16, 128), BF), v((GROUP, 16, 128), BF),
            v((RING, 16, C), BF), v((RING, 16, C), BF),
            v((GROUP, 16, WIDE), BF), v((RING, 16, WIDE), BF), v((ROWS, WIDE), BF),
            v((ROWS, INNER), F32), v((ROWS, 128), F32), v((ROWS, INNER), BF),
            dma((5,)), dma((4, 5)), dma((4, 5)), dma((2,)), dma((2,)), dma((2, 16)), dma((2, 16)),
            dma((2, 8)), dma((2, 8)), dma((2, 16)), dma((2, 16)), dma((2, 16)), dma((2, 16)),
        ],
        compiler_params=pltpu.CompilerParams(
            collective_id=0, has_side_effects=True, vmem_limit_bytes=60 * 1024 * 1024
        ),
    )(rows, w_query, w_key, w_value, w_out, halo_width, global_frame)
    return out.reshape(FRAMES, PLACES, C)


def solution(mesh):
    return jax.shard_map(
        body,
        mesh=mesh,
        in_specs=(
            P("clip", "space", None),
            P("space", None),
            P("space", None),
            P("space", None),
            P("space", None),
            P("clip"),
            P("clip"),
        ),
        out_specs=P("clip", "space", None),
        check_vma=False,
    )
```

```python
import jax
import jax.numpy as jnp
from jax import lax
from jax.experimental import pallas as pl
from jax.experimental.pallas import tpu as pltpu
from jax.sharding import PartitionSpec as P

MESH = pl.DeviceIdType.MESH
BF = jnp.bfloat16
F32 = jnp.float32

RING = 8
C = 1280
INNER = 640
FRAMES = 16
PLACES = 24
ROWS = FRAMES * PLACES
HALO = 4
PAIRS = 5
SCALE = 0.125
LOW = -1e30
SPOTS = ((0, 0), (0, 1), (1, 0))
WIDE = INNER + 128


def iota(shape, dim):
    return lax.broadcasted_iota(jnp.int32, shape, dim)


def onehot(mask):
    return jnp.where(mask, 1.0, 0.0).astype(BF)


def dot(a, b):
    return jnp.dot(a, b, preferred_element_type=F32)


def dot_t(a, b):
    return lax.dot_general(a, b, (((1,), (1,)), ((), ())), preferred_element_type=F32)


def rem(value, size):
    return lax.rem(value, jnp.int32(size))


def kernel(
    tok_hbm, wq_hbm, wk_hbm, wv_hbm, wo_hbm, halo_s, gf_s, out_ref,
    tok, xt, htok, xht, wq, wk, wv, wo, q_own, qz, qy, k_own, v_own, k_mar, v_mar, k_pool, v_pool,
    mine, rz, ry, pool, answers, og, near_o, near_l, att,
    loc_sem, w_send, w_recv, h_send, h_recv, m_send, m_recv, r_send, r_recv, q_send, q_recv, o_send, o_recv,
):
    c = lax.axis_index("clip")
    s = lax.axis_index("space")
    z, xh, y = lax.div(c, jnp.int32(16)), rem(lax.div(c, jnp.int32(8)), 2), rem(c, 8)
    xl, core = lax.div(s, jnp.int32(2)), rem(s, 2)
    x = xh * 2 + xl

    def dev(z_, xh_, y_, s_):
        return (z_ * 16 + xh_ * 8 + y_, s_)

    mate = (c, xl * 2 + 1 - core)
    up = rem(x + 1, 4)
    down = rem(x + 3, 4)
    x_up = dev(z, lax.div(up, jnp.int32(2)), y, rem(up, 2) * 2 + core)
    x_down = dev(z, lax.div(down, jnp.int32(2)), y, rem(down, 2) * 2 + core)
    clip_next = (rem(c + 1, 128), s)
    clip_prev = (rem(c + 127, 128), s)

    def loop(start, stop, act):
        def step(d, carry):
            act(d)
            return carry

        lax.fori_loop(start, stop, step, 0)

    def ring_dev(part, place, other=0):
        xh_ = rem(xh + other, 2)
        return dev(place, xh_, y, s) if part == 0 else dev(z, xh_, place, s)

    weights = ((wq_hbm, wq), (wk_hbm, wk), (wv_hbm, wv), (wo_hbm, wo))
    tok_in = pltpu.make_async_copy(tok_hbm, tok, loc_sem.at[0])
    tok_in.start()
    barrier = pltpu.get_barrier_semaphore()

    def greet(device):
        pl.semaphore_signal(barrier, inc=1, device_id=device, device_id_type=MESH)

    for device in (mate, x_up, x_down, clip_next, clip_prev):
        greet(device)
    for part in range(2):
        loop(1, 16, lambda d, part=part: greet(ring_dev(part, rem((z, y)[part] + d, RING), lax.div(d, jnp.int32(8)))))

    def shard(i, index, half=None):
        full = weights[i][1]
        rows = full.shape[0] // 4
        if half is None:
            return full.at[pl.ds(pl.multiple_of(index * rows, 16), rows)]
        return full.at[pl.ds(pl.multiple_of(index * rows + half * (rows // 2), 16), rows // 2)]

    w_in = []
    for i in range(4):
        copy = pltpu.make_async_copy(weights[i][0], shard(i, s), loc_sem.at[1 + i])
        copy.start()
        w_in.append(copy)

    def message(part, d):
        place = rem((z, y)[part] + d, RING)
        if part == 0:
            src, dst = mine.at[pl.ds(2 * place, 2)], rz.at[xh * 8 + z]
        else:
            src, dst = mine.at[16 + place], ry.at[xh * 8 + y]
        return pltpu.make_async_remote_copy(
            src_ref=src, dst_ref=dst, send_sem=m_send.at[part, d], recv_sem=m_recv.at[part, d],
            device_id=ring_dev(part, place, lax.div(d, jnp.int32(8))), device_id_type=MESH,
        )

    def each_message(act):
        for part in range(2):
            loop(1, 16, lambda d, part=part: act(message(part, d)))

    def weight_copy(i, kind):
        rows = weights[i][0].shape[0]
        theirs = (1 - xl) * 2 + core
        if kind == 0:
            src, dst, device = weights[i][0].at[pl.ds(0, rows // 2)], shard(i, s, 0), x_up
        elif kind == 1:
            src, dst, device = weights[i][0].at[pl.ds(rows // 2, rows // 2)], shard(i, s, 1), x_down
        elif kind == 2:
            src, dst, device = weights[i][0], shard(i, s), mate
        else:
            src, dst, device = shard(i, theirs, kind - 3), shard(i, theirs, kind - 3), mate
        return pltpu.make_async_remote_copy(
            src_ref=src, dst_ref=dst, send_sem=w_send.at[i, kind], recv_sem=w_recv.at[i, kind],
            device_id=device, device_id_type=MESH,
        )

    def margin_copy(side):
        edge = HALO * PLACES
        src = tok_hbm.at[pl.ds(ROWS - edge, edge)] if side == 0 else tok_hbm.at[pl.ds(0, edge)]
        return pltpu.make_async_remote_copy(
            src_ref=src,
            dst_ref=htok.at[pl.ds(side * edge, edge)],
            send_sem=h_send.at[side],
            recv_sem=h_recv.at[side],
            device_id=clip_next if side == 0 else clip_prev,
            device_id_type=MESH,
        )

    def block_copy(part, k):
        here = (y, z)[part]
        hop = (1, 2, 7, 6, 1, 2, 7, 6)[k]
        origin = here if k < 4 else rem(here + (6 if k < 6 else 2), RING)
        place = rem(here + hop, RING)
        device = dev(z, xh, place, s) if part == 0 else dev(place, xh, y, s)
        if part == 0:
            block = pool.at[origin, k // 7] if k in (5, 7) else pool.at[origin, pl.ds(0, 2)]
        elif k in (5, 7):
            block = pool.at[origin, 2, :, pl.ds(k // 7 * (C // 2), C // 2)]
        else:
            block = pool.at[origin, 2]
        return pltpu.make_async_remote_copy(
            src_ref=block, dst_ref=block,
            send_sem=r_send.at[part, k], recv_sem=r_recv.at[part, k], device_id=device, device_id_type=MESH,
        )

    def each_block(ks, act):
        for part in range(2):
            for k in ks:
                act(block_copy(part, k))

    def query_copy(part, d):
        place = rem((z, y)[part] + d, RING)
        if part == 0:
            src, dst = q_own.at[pl.ds(pl.multiple_of(place * 32, 16), 32)], qz.at[z]
        else:
            src, dst = q_own.at[pl.ds(pl.multiple_of(256 + place * 16, 16), 16)], qy.at[y]
        return pltpu.make_async_remote_copy(
            src_ref=src, dst_ref=dst, send_sem=q_send.at[part, d], recv_sem=q_recv.at[part, d],
            device_id=ring_dev(part, place), device_id_type=MESH,
        )

    def each_query(act):
        for part in range(2):
            loop(1, RING, lambda d, part=part: act(query_copy(part, d)))

    def answer_rows(k):
        part, p = SPOTS[k]
        return pl.ds(pl.multiple_of((2 * z + p) * 16 if part == 0 else (16 + y) * 16, 16), 16)

    def reply_copy(k, d):
        part = SPOTS[k][0]
        place = rem((z, y)[part] + d, RING)
        return pltpu.make_async_remote_copy(
            src_ref=answers.at[k, place], dst_ref=og.at[answer_rows(k)],
            send_sem=o_send.at[k, d], recv_sem=o_recv.at[k, d], device_id=ring_dev(part, place), device_id_type=MESH,
        )

    def each_reply(k, act):
        loop(1, RING, lambda d: act(reply_copy(k, d)))

    pl.semaphore_wait(barrier, 15 + 15 + 5)
    for kind in range(3):
        weight_copy(0, kind).start()

    tok_in.wait()
    frame = gf_s[0]
    shape = (ROWS, ROWS)
    spread = dot(onehot(iota(shape, 1) == frame * PLACES + (iota(shape, 0) >> 4)), tok[...])
    row = iota((ROWS, 128), 0) & 15
    total = jnp.zeros((ROWS, 128), F32)
    for j in range(10):
        total = jnp.where(row == j, spread[:, 128 * j : 128 * j + 128], total)
    mine[...] = total.astype(BF).reshape(PLACES, 16, 128)
    each_message(lambda copy: copy.start())

    for i in range(1, 3):
        for kind in range(3):
            weight_copy(i, kind).start()

    shape = (ROWS, ROWS)
    turn = onehot(iota(shape, 1) == (iota(shape, 0) & 15) * PLACES + (iota(shape, 0) >> 4))
    xt[...] = dot(turn, tok[...]).astype(BF)

    rz[xh * 8 + z] = mine[pl.ds(2 * z, 2)]
    ry[xh * 8 + y] = mine[16 + y]
    each_message(lambda copy: copy.wait_recv())
    r, col = iota((160, 256), 0), iota((160, 256), 1)
    choose = onehot(((r & 15) == (col >> 4)) & ((col & 15) == (r >> 4)))
    for k, (part, p) in enumerate(SPOTS):
        rows = (rz[:, p] if part == 0 else ry[...]).reshape(256, 128)
        block = dot(choose, rows).astype(BF)
        for j in range(10):
            pool[(y, z)[part], k, :, 128 * j : 128 * j + 128] = block[16 * j : 16 * j + 16]
    each_block((1, 3, 0, 2), lambda copy: copy.start())

    def pass_on(i):
        for half in range(2):
            weight_copy(i, half).wait_recv()
            weight_copy(i, 3 + half).start()

    def whole(i):
        w_in[i].wait()
        for kind in range(2, 5):
            weight_copy(i, kind).wait_recv()

    pass_on(0)
    whole(0)
    q_own[...] = (dot(xt[...], wq[...]) * SCALE).astype(BF)
    each_query(lambda copy: copy.start())
    qz[z] = q_own[pl.ds(pl.multiple_of(z * 32, 16), 32)]
    qy[y] = q_own[pl.ds(pl.multiple_of(256 + y * 16, 16), 16)]
    each_block((1, 3), lambda copy: copy.wait_recv())
    each_block((4, 5, 6, 7), lambda copy: copy.start())

    pass_on(1)
    for kind in range(3):
        weight_copy(3, kind).start()
    whole(1)
    k_own[...] = dot(xt[...], wk[...]).astype(BF)
    pass_on(2)
    for side in range(2):
        margin_copy(side).start()
    each_block((0, 2, 4, 5, 6, 7), lambda copy: copy.wait_recv())
    k_pool[...] = dot(pool[...].reshape(ROWS, C), wk[...]).astype(BF).reshape(RING, 3, 16, INNER)
    whole(2)
    v_pool[...] = dot(pool[...].reshape(ROWS, C), wv[...]).astype(BF).reshape(RING, 3, 16, INNER)

    lane = iota((128, 128), 1)
    left = lane < 64
    left_b = onehot(iota((1, 128), 1) < 64)
    right_b = onehot(iota((1, 128), 1) >= 64)
    each_query(lambda copy: copy.wait_recv())

    for k, (part, p) in enumerate(SPOTS):
        queries = (qz, qy)[part]
        logs = jnp.zeros((128, 128), F32)
        for pair in range(PAIRS):
            lanes = slice(128 * pair, 128 * pair + 128)
            q = queries[:, 16 * p : 16 * p + 16, lanes].reshape(128, 128)
            keys = k_pool[:, k, :, lanes].reshape(128, 128)
            values = v_pool[:, k, :, lanes].reshape(128, 128)
            scores = dot_t(q, jnp.concatenate([keys * left_b, keys * right_b], axis=0))
            s0, s1 = scores[:, :128], scores[:, 128:]
            m0 = jnp.max(s0, axis=1, keepdims=True)
            m1 = jnp.max(s1, axis=1, keepdims=True)
            e0 = jnp.exp(s0 - m0)
            e1 = jnp.exp(s1 - m1)
            l0 = jnp.sum(e0, axis=1, keepdims=True)
            l1 = jnp.sum(e1, axis=1, keepdims=True)
            mixed = dot(
                jnp.concatenate([e0.astype(BF), e1.astype(BF)], axis=1),
                jnp.concatenate([values * left_b, values * right_b], axis=0),
            )
            mixed = mixed * jnp.where(left, 1.0 / l0, 1.0 / l1)
            answers[k, :, :, lanes] = mixed.astype(BF).reshape(RING, 16, 128)
            logs = jnp.where(lane == 2 * pair, m0 + jnp.log(l0), logs)
            logs = jnp.where(lane == 2 * pair + 1, m1 + jnp.log(l1), logs)
        high = logs.astype(BF).astype(F32)
        middle = (logs - high).astype(BF).astype(F32)
        low = (logs - high - middle).astype(BF).astype(F32)
        packed = high + pltpu.roll(middle, 16, 1) + pltpu.roll(low, 32, 1)
        answers[k, :, :, INNER:] = packed.astype(BF).reshape(RING, 16, 128)
        each_reply(k, lambda copy: copy.start())
        og[answer_rows(k)] = answers[k, (z, y)[part]]

    v_own[...] = dot(xt[...], wv[...]).astype(BF)
    pass_on(3)

    for side in range(2):
        margin_copy(side).wait_recv()
    edge = 2 * HALO * PLACES
    shape = (edge, edge)
    turn = onehot(iota(shape, 1) == (iota(shape, 0) & 7) * PLACES + (iota(shape, 0) >> 3))
    xht[...] = dot(turn, htok[...]).astype(BF)
    k_mar[...] = dot(xht[...], wk[...]).astype(BF)
    v_mar[...] = dot(xht[...], wv[...]).astype(BF)

    row8 = iota((128, 128), 0) >> 4
    own_bias = jnp.where(row8 == (lane >> 4), 0.0, LOW)
    half = lane & 63
    slot = half & 7
    reach = halo_s[0]
    before = (slot < HALO) & (c > 0) & (HALO - slot <= reach)
    after = (slot >= HALO) & (c < 127) & (slot - HALO + 1 <= reach)
    mar_bias = jnp.where((row8 == (half >> 3)) & (before | after), 0.0, LOW)
    for g in range(3):
        rows = slice(128 * g, 128 * g + 128)
        edges = slice(64 * g, 64 * g + 64)
        logs = jnp.zeros((128, 128), F32)
        for pair in range(PAIRS):
            lanes = slice(128 * pair, 128 * pair + 128)
            q = q_own[rows, lanes]
            ko, vo, km, vm = k_own[rows, lanes], v_own[rows, lanes], k_mar[edges, lanes], v_mar[edges, lanes]
            scores = dot_t(q, jnp.concatenate([ko * left_b, ko * right_b, km * left_b, km * right_b], axis=0))
            s0 = scores[:, :128] + own_bias
            s1 = scores[:, 128:256] + own_bias
            sm = scores[:, 256:] + mar_bias
            m0 = jnp.max(jnp.maximum(s0, jnp.where(left, sm, LOW)), axis=1, keepdims=True)
            m1 = jnp.max(jnp.maximum(s1, jnp.where(left, LOW, sm)), axis=1, keepdims=True)
            e0 = jnp.exp(s0 - m0)
            e1 = jnp.exp(s1 - m1)
            em = jnp.exp(sm - jnp.where(left, m0, m1))
            l0 = jnp.sum(e0 + jnp.where(left, em, 0.0), axis=1, keepdims=True)
            l1 = jnp.sum(e1 + jnp.where(left, 0.0, em), axis=1, keepdims=True)
            mixed = dot(
                jnp.concatenate([e0.astype(BF), e1.astype(BF), em.astype(BF)], axis=1),
                jnp.concatenate([vo * left_b, vo * right_b, vm * left_b, vm * right_b], axis=0),
            )
            near_o[rows, lanes] = mixed * jnp.where(left, 1.0 / l0, 1.0 / l1)
            logs = jnp.where(lane == 2 * pair, m0 + jnp.log(l0), logs)
            logs = jnp.where(lane == 2 * pair + 1, m1 + jnp.log(l1), logs)
        near_l[rows, :] = logs

    each_message(lambda copy: copy.wait_send())
    for i in range(3):
        for kind in range(5):
            weight_copy(i, kind).wait_send()
    for side in range(2):
        margin_copy(side).wait_send()
    each_block(range(8), lambda copy: copy.wait_send())
    each_query(lambda copy: copy.wait_send())

    for k in range(3):
        each_reply(k, lambda copy: copy.wait_recv())
    r128, c128 = iota((128, 128), 0), iota((128, 128), 1)
    gather_logs = onehot(((r128 & 15) == c128) & (r128 < 48) & (c128 < 10))
    expand = onehot(iota((128, INNER), 0) == (iota((128, INNER), 1) >> 6))
    for g in range(3):
        rows = slice(128 * g, 128 * g + 128)
        far_l = dot(og[rows, INNER:], gather_logs)
        share = 1.0 / (1.0 + jnp.exp(near_l[rows, :] - far_l))
        high = share.astype(BF)
        rest = (share - high.astype(F32)).astype(BF)
        wide = dot(high, expand) + dot(rest, expand)
        near = near_o[rows, :]
        att[rows, :] = (near + wide * (og[rows, :INNER].astype(F32) - near)).astype(BF)
    shape = (ROWS, ROWS)
    turn = onehot(iota(shape, 0) == (iota(shape, 1) & 15) * PLACES + (iota(shape, 1) >> 4))
    ordered = dot(turn, att[...]).astype(BF)
    whole(3)
    out_ref[...] = dot(ordered, wo[...]).astype(BF)

    for kind in range(5):
        weight_copy(3, kind).wait_send()
    for k in range(3):
        each_reply(k, lambda copy: copy.wait_send())


def body(tokens, w_query, w_key, w_value, w_out, halo_width, global_frame):
    rows = tokens.reshape(ROWS, C)
    any_spec = pl.BlockSpec(memory_space=pl.ANY)
    smem = pl.BlockSpec(memory_space=pltpu.SMEM)
    v = pltpu.VMEM
    dma = pltpu.SemaphoreType.DMA
    edge = 2 * HALO * PLACES
    out = pl.pallas_call(
        kernel,
        out_shape=jax.ShapeDtypeStruct((ROWS, C), BF),
        in_specs=[any_spec] * 5 + [smem] * 2,
        out_specs=pl.BlockSpec(memory_space=pltpu.VMEM),
        scratch_shapes=[
            v((ROWS, C), BF), v((ROWS, C), BF), v((edge, C), BF), v((edge, C), BF),
            v((C, INNER), BF), v((C, INNER), BF), v((C, INNER), BF), v((INNER, C), BF),
            v((ROWS, INNER), BF), v((RING, 32, INNER), BF), v((RING, 16, INNER), BF),
            v((ROWS, INNER), BF), v((ROWS, INNER), BF), v((edge, INNER), BF), v((edge, INNER), BF),
            v((RING, 3, 16, INNER), BF), v((RING, 3, 16, INNER), BF),
            v((PLACES, 16, 128), BF), v((16, 2, 16, 128), BF), v((16, 16, 128), BF),
            v((RING, 3, 16, C), BF),
            v((3, RING, 16, WIDE), BF), v((ROWS, WIDE), BF),
            v((ROWS, INNER), F32), v((ROWS, 128), F32), v((ROWS, INNER), BF),
            dma((5,)), dma((4, 5)), dma((4, 5)), dma((2,)), dma((2,)), dma((2, 16)), dma((2, 16)),
            dma((2, 8)), dma((2, 8)), dma((2, 8)), dma((2, 8)), dma((3, 8)), dma((3, 8)),
        ],
        compiler_params=pltpu.CompilerParams(
            collective_id=0, has_side_effects=True, vmem_limit_bytes=60 * 1024 * 1024
        ),
    )(rows, w_query, w_key, w_value, w_out, halo_width, global_frame)
    return out.reshape(FRAMES, PLACES, C)


def solution(mesh):
    return jax.shard_map(
        body,
        mesh=mesh,
        in_specs=(
            P("clip", "space", None),
            P("space", None),
            P("space", None),
            P("space", None),
            P("space", None),
            P("clip"),
            P("clip"),
        ),
        out_specs=P("clip", "space", None),
        check_vma=False,
    )
```

```python
import jax
import jax.numpy as jnp
from jax import lax
from jax.experimental import pallas as pl
from jax.experimental.pallas import tpu as pltpu
from jax.sharding import PartitionSpec as P

MESH = pl.DeviceIdType.MESH
BF = jnp.bfloat16
F32 = jnp.float32

RING = 8
C = 1280
INNER = 640
FRAMES = 16
PLACES = 24
ROWS = FRAMES * PLACES
HALO = 4
PAIRS = 5
SCALE = 0.125
LOW = -1e30
SPOTS = ((0, 0), (0, 1), (1, 0))
WIDE = INNER + 128


def iota(shape, dim):
    return lax.broadcasted_iota(jnp.int32, shape, dim)


def onehot(mask):
    return jnp.where(mask, 1.0, 0.0).astype(BF)


def dot(a, b):
    return jnp.dot(a, b, preferred_element_type=F32)


def dot_t(a, b):
    return lax.dot_general(a, b, (((1,), (1,)), ((), ())), preferred_element_type=F32)


def rem(value, size):
    return lax.rem(value, jnp.int32(size))


def kernel(
    tok_hbm, wq_hbm, wk_hbm, wv_hbm, wo_hbm, halo_s, gf_s, out_ref,
    tok, xt, htok, xht, wq, wk, wv, wo, q_own, qz, qy, k_own, v_own, k_mar, v_mar, k_pool, v_pool,
    mine, rz, ry, pool, answers, og, near_o, near_l, att,
    loc_sem, w_send, w_recv, h_send, h_recv, m_send, m_recv, r_send, r_recv, q_send, q_recv, o_send, o_recv,
):
    c = lax.axis_index("clip")
    s = lax.axis_index("space")
    z, xh, y = lax.div(c, jnp.int32(16)), rem(lax.div(c, jnp.int32(8)), 2), rem(c, 8)
    xl, core = lax.div(s, jnp.int32(2)), rem(s, 2)
    x = xh * 2 + xl

    def dev(z_, xh_, y_, s_):
        return (z_ * 16 + xh_ * 8 + y_, s_)

    mate = (c, xl * 2 + 1 - core)
    up = rem(x + 1, 4)
    down = rem(x + 3, 4)
    x_up = dev(z, lax.div(up, jnp.int32(2)), y, rem(up, 2) * 2 + core)
    x_down = dev(z, lax.div(down, jnp.int32(2)), y, rem(down, 2) * 2 + core)
    clip_next = (rem(c + 1, 128), s)
    clip_prev = (rem(c + 127, 128), s)

    def loop(start, stop, act):
        def step(d, carry):
            act(d)
            return carry

        lax.fori_loop(start, stop, step, 0)

    def ring_dev(part, place, other=0):
        xh_ = rem(xh + other, 2)
        return dev(place, xh_, y, s) if part == 0 else dev(z, xh_, place, s)

    weights = ((wq_hbm, wq), (wk_hbm, wk), (wv_hbm, wv), (wo_hbm, wo))
    tok_in = pltpu.make_async_copy(tok_hbm, tok, loc_sem.at[0])
    tok_in.start()
    barrier = pltpu.get_barrier_semaphore()

    def greet(device):
        pl.semaphore_signal(barrier, inc=1, device_id=device, device_id_type=MESH)

    for device in (mate, x_up, x_down, clip_next, clip_prev):
        greet(device)
    for part in range(2):
        loop(1, 16, lambda d, part=part: greet(ring_dev(part, rem((z, y)[part] + d, RING), lax.div(d, jnp.int32(8)))))

    def shard(i, index, half=None):
        full = weights[i][1]
        rows = full.shape[0] // 4
        if half is None:
            return full.at[pl.ds(pl.multiple_of(index * rows, 16), rows)]
        return full.at[pl.ds(pl.multiple_of(index * rows + half * (rows // 2), 16), rows // 2)]

    w_in = []
    for i in range(4):
        copy = pltpu.make_async_copy(weights[i][0], shard(i, s), loc_sem.at[1 + i])
        copy.start()
        w_in.append(copy)

    def message(part, d):
        place = rem((z, y)[part] + d, RING)
        if part == 0:
            src, dst = mine.at[pl.ds(2 * place, 2)], rz.at[xh * 8 + z]
        else:
            src, dst = mine.at[16 + place], ry.at[xh * 8 + y]
        return pltpu.make_async_remote_copy(
            src_ref=src, dst_ref=dst, send_sem=m_send.at[part, d], recv_sem=m_recv.at[part, d],
            device_id=ring_dev(part, place, lax.div(d, jnp.int32(8))), device_id_type=MESH,
        )

    def each_message(act):
        for part in range(2):
            loop(1, 16, lambda d, part=part: act(message(part, d)))

    def weight_copy(i, kind):
        rows = weights[i][0].shape[0]
        theirs = (1 - xl) * 2 + core
        if kind == 0:
            src, dst, device = weights[i][0].at[pl.ds(0, rows // 2)], shard(i, s, 0), x_up
        elif kind == 1:
            src, dst, device = weights[i][0].at[pl.ds(rows // 2, rows // 2)], shard(i, s, 1), x_down
        elif kind == 2:
            src, dst, device = weights[i][0], shard(i, s), mate
        else:
            src, dst, device = shard(i, theirs, kind - 3), shard(i, theirs, kind - 3), mate
        return pltpu.make_async_remote_copy(
            src_ref=src, dst_ref=dst, send_sem=w_send.at[i, kind], recv_sem=w_recv.at[i, kind],
            device_id=device, device_id_type=MESH,
        )

    def margin_copy(side):
        edge = HALO * PLACES
        src = tok_hbm.at[pl.ds(ROWS - edge, edge)] if side == 0 else tok_hbm.at[pl.ds(0, edge)]
        return pltpu.make_async_remote_copy(
            src_ref=src,
            dst_ref=htok.at[pl.ds(side * edge, edge)],
            send_sem=h_send.at[side],
            recv_sem=h_recv.at[side],
            device_id=clip_next if side == 0 else clip_prev,
            device_id_type=MESH,
        )

    def block_copy(part, k):
        here = (y, z)[part]
        hop = (1, 2, 7, 6, 1, 2, 7, 6)[k]
        origin = here if k < 4 else rem(here + (6 if k < 6 else 2), RING)
        place = rem(here + hop, RING)
        device = dev(z, xh, place, s) if part == 0 else dev(place, xh, y, s)
        if part == 0:
            block = pool.at[origin, k // 7] if k in (5, 7) else pool.at[origin, pl.ds(0, 2)]
        elif k in (5, 7):
            block = pool.at[origin, 2, :, pl.ds(k // 7 * (C // 2), C // 2)]
        else:
            block = pool.at[origin, 2]
        return pltpu.make_async_remote_copy(
            src_ref=block, dst_ref=block,
            send_sem=r_send.at[part, k], recv_sem=r_recv.at[part, k], device_id=device, device_id_type=MESH,
        )

    def each_block(ks, act):
        for part in range(2):
            for k in ks:
                act(block_copy(part, k))

    def query_copy(part, d):
        place = rem((z, y)[part] + d, RING)
        if part == 0:
            src, dst = q_own.at[pl.ds(pl.multiple_of(place * 32, 16), 32)], qz.at[z]
        else:
            src, dst = q_own.at[pl.ds(pl.multiple_of(256 + place * 16, 16), 16)], qy.at[y]
        return pltpu.make_async_remote_copy(
            src_ref=src, dst_ref=dst, send_sem=q_send.at[part, d], recv_sem=q_recv.at[part, d],
            device_id=ring_dev(part, place), device_id_type=MESH,
        )

    def each_query(act):
        for part in range(2):
            loop(1, RING, lambda d, part=part: act(query_copy(part, d)))

    def answer_rows(k):
        part, p = SPOTS[k]
        return pl.ds(pl.multiple_of((2 * z + p) * 16 if part == 0 else (16 + y) * 16, 16), 16)

    def reply_copy(k, d):
        part = SPOTS[k][0]
        place = rem((z, y)[part] + d, RING)
        return pltpu.make_async_remote_copy(
            src_ref=answers.at[k, place], dst_ref=og.at[answer_rows(k)],
            send_sem=o_send.at[k, d], recv_sem=o_recv.at[k, d], device_id=ring_dev(part, place), device_id_type=MESH,
        )

    def each_reply(k, act):
        loop(1, RING, lambda d: act(reply_copy(k, d)))

    pl.semaphore_wait(barrier, 15 + 15 + 5)
    for kind in range(3):
        weight_copy(0, kind).start()

    tok_in.wait()
    frame = gf_s[0]
    shape = (ROWS, ROWS)
    spread = dot(onehot(iota(shape, 1) == frame * PLACES + (iota(shape, 0) >> 4)), tok[...])
    row = iota((ROWS, 128), 0) & 15
    total = jnp.zeros((ROWS, 128), F32)
    for j in range(10):
        total = jnp.where(row == j, spread[:, 128 * j : 128 * j + 128], total)
    mine[...] = total.astype(BF).reshape(PLACES, 16, 128)
    each_message(lambda copy: copy.start())

    for i in range(1, 3):
        for kind in range(3):
            weight_copy(i, kind).start()

    shape = (ROWS, ROWS)
    turn = onehot(iota(shape, 1) == (iota(shape, 0) & 15) * PLACES + (iota(shape, 0) >> 4))
    xt[...] = dot(turn, tok[...]).astype(BF)

    rz[xh * 8 + z] = mine[pl.ds(2 * z, 2)]
    ry[xh * 8 + y] = mine[16 + y]
    each_message(lambda copy: copy.wait_recv())
    r, col = iota((160, 256), 0), iota((160, 256), 1)
    choose = onehot(((r & 15) == (col >> 4)) & ((col & 15) == (r >> 4)))
    for k, (part, p) in enumerate(SPOTS):
        rows = (rz[:, p] if part == 0 else ry[...]).reshape(256, 128)
        block = dot(choose, rows).astype(BF)
        for j in range(10):
            pool[(y, z)[part], k, :, 128 * j : 128 * j + 128] = block[16 * j : 16 * j + 16]
    each_block((1, 3, 0, 2), lambda copy: copy.start())

    def pass_on(i):
        for half in range(2):
            weight_copy(i, half).wait_recv()
            weight_copy(i, 3 + half).start()

    def whole(i):
        w_in[i].wait()
        for kind in range(2, 5):
            weight_copy(i, kind).wait_recv()

    pass_on(0)
    whole(0)
    q_own[...] = (dot(xt[...], wq[...]) * SCALE).astype(BF)
    each_query(lambda copy: copy.start())
    qz[z] = q_own[pl.ds(pl.multiple_of(z * 32, 16), 32)]
    qy[y] = q_own[pl.ds(pl.multiple_of(256 + y * 16, 16), 16)]
    each_block((1, 3), lambda copy: copy.wait_recv())
    each_block((4, 5, 6, 7), lambda copy: copy.start())

    pass_on(1)
    for kind in range(3):
        weight_copy(3, kind).start()
    whole(1)
    for side in range(2):
        margin_copy(side).start()
    k_own[...] = dot(xt[...], wk[...]).astype(BF)
    pass_on(2)
    each_block((0, 2, 4, 5, 6, 7), lambda copy: copy.wait_recv())
    k_pool[...] = dot(pool[...].reshape(ROWS, C), wk[...]).astype(BF).reshape(RING, 3, 16, INNER)
    whole(2)
    v_pool[...] = dot(pool[...].reshape(ROWS, C), wv[...]).astype(BF).reshape(RING, 3, 16, INNER)

    lane = iota((128, 128), 1)
    left = lane < 64
    left_b = onehot(iota((1, 128), 1) < 64)
    right_b = onehot(iota((1, 128), 1) >= 64)

    for k in (2, 0, 1):
        part, p = SPOTS[k]
        if k != 1:
            loop(1, RING, lambda d, part=part: query_copy(part, d).wait_recv())
        queries = (qz, qy)[part]
        logs = jnp.zeros((128, 128), F32)
        for pair in range(PAIRS):
            lanes = slice(128 * pair, 128 * pair + 128)
            q = queries[:, 16 * p : 16 * p + 16, lanes].reshape(128, 128)
            keys = k_pool[:, k, :, lanes].reshape(128, 128)
            values = v_pool[:, k, :, lanes].reshape(128, 128)
            scores = dot_t(q, jnp.concatenate([keys * left_b, keys * right_b], axis=0))
            s0, s1 = scores[:, :128], scores[:, 128:]
            m0 = jnp.max(s0, axis=1, keepdims=True)
            m1 = jnp.max(s1, axis=1, keepdims=True)
            e0 = jnp.exp(s0 - m0)
            e1 = jnp.exp(s1 - m1)
            l0 = jnp.sum(e0, axis=1, keepdims=True)
            l1 = jnp.sum(e1, axis=1, keepdims=True)
            mixed = dot(
                jnp.concatenate([e0.astype(BF), e1.astype(BF)], axis=1),
                jnp.concatenate([values * left_b, values * right_b], axis=0),
            )
            mixed = mixed * jnp.where(left, 1.0 / l0, 1.0 / l1)
            answers[k, :, :, lanes] = mixed.astype(BF).reshape(RING, 16, 128)
            logs = jnp.where(lane == 2 * pair, m0 + jnp.log(l0), logs)
            logs = jnp.where(lane == 2 * pair + 1, m1 + jnp.log(l1), logs)
        high = logs.astype(BF).astype(F32)
        middle = (logs - high).astype(BF).astype(F32)
        low = (logs - high - middle).astype(BF).astype(F32)
        packed = high + pltpu.roll(middle, 16, 1) + pltpu.roll(low, 32, 1)
        answers[k, :, :, INNER:] = packed.astype(BF).reshape(RING, 16, 128)
        each_reply(k, lambda copy: copy.start())
        og[answer_rows(k)] = answers[k, (z, y)[part]]

    v_own[...] = dot(xt[...], wv[...]).astype(BF)

    for side in range(2):
        margin_copy(side).wait_recv()
    edge = 2 * HALO * PLACES
    shape = (edge, edge)
    turn = onehot(iota(shape, 1) == (iota(shape, 0) & 7) * PLACES + (iota(shape, 0) >> 3))
    xht[...] = dot(turn, htok[...]).astype(BF)
    k_mar[...] = dot(xht[...], wk[...]).astype(BF)
    v_mar[...] = dot(xht[...], wv[...]).astype(BF)

    row8 = iota((128, 128), 0) >> 4
    own_bias = jnp.where(row8 == (lane >> 4), 0.0, LOW)
    half = lane & 63
    slot = half & 7
    reach = halo_s[0]
    before = (slot < HALO) & (c > 0) & (HALO - slot <= reach)
    after = (slot >= HALO) & (c < 127) & (slot - HALO + 1 <= reach)
    mar_bias = jnp.where((row8 == (half >> 3)) & (before | after), 0.0, LOW)
    for g in range(3):
        rows = slice(128 * g, 128 * g + 128)
        edges = slice(64 * g, 64 * g + 64)
        logs = jnp.zeros((128, 128), F32)
        for pair in range(PAIRS):
            lanes = slice(128 * pair, 128 * pair + 128)
            q = q_own[rows, lanes]
            ko, vo, km, vm = k_own[rows, lanes], v_own[rows, lanes], k_mar[edges, lanes], v_mar[edges, lanes]
            scores = dot_t(q, jnp.concatenate([ko * left_b, ko * right_b, km * left_b, km * right_b], axis=0))
            s0 = scores[:, :128] + own_bias
            s1 = scores[:, 128:256] + own_bias
            sm = scores[:, 256:] + mar_bias
            m0 = jnp.max(jnp.maximum(s0, jnp.where(left, sm, LOW)), axis=1, keepdims=True)
            m1 = jnp.max(jnp.maximum(s1, jnp.where(left, LOW, sm)), axis=1, keepdims=True)
            e0 = jnp.exp(s0 - m0)
            e1 = jnp.exp(s1 - m1)
            em = jnp.exp(sm - jnp.where(left, m0, m1))
            l0 = jnp.sum(e0 + jnp.where(left, em, 0.0), axis=1, keepdims=True)
            l1 = jnp.sum(e1 + jnp.where(left, 0.0, em), axis=1, keepdims=True)
            mixed = dot(
                jnp.concatenate([e0.astype(BF), e1.astype(BF), em.astype(BF)], axis=1),
                jnp.concatenate([vo * left_b, vo * right_b, vm * left_b, vm * right_b], axis=0),
            )
            near_o[rows, lanes] = mixed * jnp.where(left, 1.0 / l0, 1.0 / l1)
            logs = jnp.where(lane == 2 * pair, m0 + jnp.log(l0), logs)
            logs = jnp.where(lane == 2 * pair + 1, m1 + jnp.log(l1), logs)
        near_l[rows, :] = logs

    pass_on(3)
    each_message(lambda copy: copy.wait_send())
    for i in range(3):
        for kind in range(5):
            weight_copy(i, kind).wait_send()
    for side in range(2):
        margin_copy(side).wait_send()
    each_block(range(8), lambda copy: copy.wait_send())
    each_query(lambda copy: copy.wait_send())

    for k in range(3):
        each_reply(k, lambda copy: copy.wait_recv())
    r128, c128 = iota((128, 128), 0), iota((128, 128), 1)
    gather_logs = onehot(((r128 & 15) == c128) & (r128 < 48) & (c128 < 10))
    expand = onehot(iota((128, INNER), 0) == (iota((128, INNER), 1) >> 6))
    for g in range(3):
        rows = slice(128 * g, 128 * g + 128)
        far_l = dot(og[rows, INNER:], gather_logs)
        share = 1.0 / (1.0 + jnp.exp(near_l[rows, :] - far_l))
        high = share.astype(BF)
        rest = (share - high.astype(F32)).astype(BF)
        wide = dot(high, expand) + dot(rest, expand)
        near = near_o[rows, :]
        att[rows, :] = (near + wide * (og[rows, :INNER].astype(F32) - near)).astype(BF)
    shape = (ROWS, ROWS)
    turn = onehot(iota(shape, 0) == (iota(shape, 1) & 15) * PLACES + (iota(shape, 1) >> 4))
    ordered = dot(turn, att[...]).astype(BF)
    whole(3)
    out_ref[...] = dot(ordered, wo[...]).astype(BF)

    for kind in range(5):
        weight_copy(3, kind).wait_send()
    for k in range(3):
        each_reply(k, lambda copy: copy.wait_send())


def body(tokens, w_query, w_key, w_value, w_out, halo_width, global_frame):
    rows = tokens.reshape(ROWS, C)
    any_spec = pl.BlockSpec(memory_space=pl.ANY)
    smem = pl.BlockSpec(memory_space=pltpu.SMEM)
    v = pltpu.VMEM
    dma = pltpu.SemaphoreType.DMA
    edge = 2 * HALO * PLACES
    out = pl.pallas_call(
        kernel,
        out_shape=jax.ShapeDtypeStruct((ROWS, C), BF),
        in_specs=[any_spec] * 5 + [smem] * 2,
        out_specs=pl.BlockSpec(memory_space=pltpu.VMEM),
        scratch_shapes=[
            v((ROWS, C), BF), v((ROWS, C), BF), v((edge, C), BF), v((edge, C), BF),
            v((C, INNER), BF), v((C, INNER), BF), v((C, INNER), BF), v((INNER, C), BF),
            v((ROWS, INNER), BF), v((RING, 32, INNER), BF), v((RING, 16, INNER), BF),
            v((ROWS, INNER), BF), v((ROWS, INNER), BF), v((edge, INNER), BF), v((edge, INNER), BF),
            v((RING, 3, 16, INNER), BF), v((RING, 3, 16, INNER), BF),
            v((PLACES, 16, 128), BF), v((16, 2, 16, 128), BF), v((16, 16, 128), BF),
            v((RING, 3, 16, C), BF),
            v((3, RING, 16, WIDE), BF), v((ROWS, WIDE), BF),
            v((ROWS, INNER), F32), v((ROWS, 128), F32), v((ROWS, INNER), BF),
            dma((5,)), dma((4, 5)), dma((4, 5)), dma((2,)), dma((2,)), dma((2, 16)), dma((2, 16)),
            dma((2, 8)), dma((2, 8)), dma((2, 8)), dma((2, 8)), dma((3, 8)), dma((3, 8)),
        ],
        compiler_params=pltpu.CompilerParams(
            collective_id=0, has_side_effects=True, vmem_limit_bytes=60 * 1024 * 1024
        ),
    )(rows, w_query, w_key, w_value, w_out, halo_width, global_frame)
    return out.reshape(FRAMES, PLACES, C)


def solution(mesh):
    return jax.shard_map(
        body,
        mesh=mesh,
        in_specs=(
            P("clip", "space", None),
            P("space", None),
            P("space", None),
            P("space", None),
            P("space", None),
            P("clip"),
            P("clip"),
        ),
        out_specs=P("clip", "space", None),
        check_vma=False,
    )
```
